512 devices in a mesh: dp: 32 (over y_lo, z), tensor: 16 (over x, y_hi, core).
Axes of the slice: x: 4, y: 8 (y_hi: 2, y_lo: 4; y = y_hi * 4 + y_lo), z: 8, core: 2. Of those that a mesh axis runs over, the one named last changes fastest.
Arguments:
- q_latent: bfloat16 [32768, 1536], P(('dp', 'tensor')), parts along dimension 0, may hold values from -150 to 150
- kv_latent: bfloat16 [32768, 576], P(('dp', 'tensor')), parts along dimension 0, may hold values from -700 to 700
- q_gain: float32 [1536], replicated, may hold values from 0.1 to 1.9
- kv_gain: float32 [512], replicated, may hold values from 0.1 to 1.9
- w_q_up: bfloat16 [1536, 12288], P(None, 'tensor'), may hold values from -0.25 to 0.25
- w_kv_up: bfloat16 [512, 16384], P(None, 'tensor'), may hold values from -0.4375 to 0.4375
Outputs:
- attended: bfloat16 [32768, 8192], P(('dp', 'tensor')), parts along dimension 0
The draws below stay inside these ranges and needn't reach their ends.
There are 32 independent parts, one for each index of `dp`. The reference program is written for one: setup_inputs(seed, part) draws one part's arguments, and reference() takes and returns one part's arrays. A program takes and returns all parts, laid end to end along the dimension named above; an argument that names none is the same for every part. Nothing has to cross between parts.
All inputs are finite; a program needn't handle non-finite values.
Results may differ from the reference program's by a relative error of at most 0.03.
Values may be sent and summed in bfloat16 or wider, within the bound.
A program may use at most 64 MiB of HBM per device.

```python
import jax
import jax.numpy as jnp
from jax import lax

Q_LAT = 1536
KV_LAT = 512
ROPE = 64
NOPE = 128
VDIM = 128
HEADS = 64
SEQ = 1024


def scale_draw(key, count, lowest, highest):
    return jnp.exp(jax.random.uniform(key, (count,), jnp.float32, jnp.log(lowest), jnp.log(highest)))


def latent_draw(key, row_count, width, noise, highest):
    row_key, column_key = jax.random.split(key, 2)
    row_scales = scale_draw(row_key, row_count, 1.0, highest)[:, None]
    column_scales = scale_draw(column_key, width, 1.0 / 3.0, 3.0)[None, :]
    return noise * row_scales * column_scales


def draw_q_latent(key, part):
    key = jax.random.fold_in(key, 11)
    scale_key, noise_key = jax.random.split(key, 2)
    noise = jnp.clip(jax.random.normal(noise_key, (SEQ, Q_LAT), jnp.float32), -4.0, 4.0)
    highest = 10.0
    return latent_draw(scale_key, SEQ, Q_LAT, noise, highest).astype(jnp.bfloat16)


def draw_kv_latent(key, part):
    key = jax.random.fold_in(key, 12)
    scale_key = jax.random.fold_in(key, 0)
    noise_key = jax.random.fold_in(key, 1)
    rope_key = jax.random.fold_in(key, 3)
    noise = jnp.clip(jax.random.normal(noise_key, (SEQ, KV_LAT), jnp.float32), -4.0, 4.0)
    highest = 10.0
    rotary = jnp.clip(jax.random.normal(rope_key, (SEQ, ROPE), jnp.float32), -4.0, 4.0)
    latent = latent_draw(scale_key, SEQ, KV_LAT, noise, highest)
    return jnp.concatenate([latent, rotary], axis=1).astype(jnp.bfloat16)


def level_of(rng, dims, shards, smallest, high):
    level = 1.0
    for position, shards_of in shards:
        heights = jax.random.uniform(jax.random.fold_in(jax.random.fold_in(rng, 6), position), (shards_of,), jnp.float32, smallest / len(shards), high / len(shards))
        level = level * jnp.repeat(jnp.exp(heights), dims[position] // shards_of).reshape((-1,) + (1,) * (len(dims) - 1 - position))
    return level


def bell_draw(key, shape, deviation, reach, cuts=(), kind=jnp.bfloat16):
    result = jax.random.normal(key, shape, jnp.float32) * deviation
    if len(cuts) > 0:
        result = level_of(key, shape, cuts, -0.22, 0.18) * result
    return jnp.clip(result, min=-reach, max=reach).astype(kind)


def setup_inputs(seed: int = 0, part: int = 0) -> dict:
    arg_keys = jax.random.split(jax.random.key(seed), 7)
    own_keys = jax.random.split(jax.random.fold_in(arg_keys[6], part), 7)
    return {
        "q_latent": draw_q_latent(jax.random.fold_in(jax.random.fold_in(arg_keys[6], part), 71), part),
        "kv_latent": draw_kv_latent(jax.random.fold_in(jax.random.fold_in(arg_keys[6], part), 71), part),
        "q_gain": jnp.clip(1.0 + 0.18 * jax.random.normal(arg_keys[2], (Q_LAT,), jnp.float32), 0.1, 1.9),
        "kv_gain": jnp.clip(1.0 + 0.18 * jax.random.normal(arg_keys[3], (KV_LAT,), jnp.float32), 0.1, 1.9),
        "w_q_up": bell_draw(arg_keys[4], (Q_LAT, HEADS * (NOPE + ROPE)), (Q_LAT // 3) ** -0.5, 0.25, ((1, 16),)),
        "w_kv_up": bell_draw(arg_keys[5], (KV_LAT, HEADS * (NOPE + VDIM)), (KV_LAT // 3) ** -0.5, 0.4375, ((1, 16),)),
    }


EPSILON = 1e-06

def normalize(latent, gain_vector):
    widened = latent.astype(jnp.float32)
    mean_square = lax.optimization_barrier(jnp.mean(widened * widened, axis=-1, keepdims=True))
    return (widened * lax.rsqrt(mean_square + EPSILON) * gain_vector).astype(jnp.bfloat16)

def angle_tables(positions, width):
    half_width = width // 2
    exponent = jnp.arange(half_width, dtype=jnp.float32) * (2.0 / width)
    frequency = jnp.power(10000.0, -exponent)
    angles = positions[:, None] * frequency[None, :]
    return (jnp.cos(angles), jnp.sin(angles))

def rotate(vectors, cosine_table, sine_table):
    half_width = vectors.shape[-1] // 2
    first_half = vectors[..., :half_width]
    second_half = vectors[..., half_width:]
    return jnp.concatenate([first_half * cosine_table - second_half * sine_table, second_half * cosine_table + first_half * sine_table], axis=-1)

def reference(q_latent, kv_latent, q_gain, kv_gain, w_q_up, w_kv_up):
    length = q_latent.shape[0]
    positions = jnp.arange(length, dtype=jnp.float32)
    cosine_table, sine_table = angle_tables(positions, ROPE)
    q_normed = normalize(q_latent, q_gain)
    kv_normed = normalize(kv_latent[:, :KV_LAT], kv_gain)
    key_rope = rotate(kv_latent[:, KV_LAT:].astype(jnp.float32), cosine_table, sine_table).astype(jnp.bfloat16)
    projected = jnp.dot(q_normed, w_q_up, preferred_element_type=jnp.float32).reshape(length, HEADS, NOPE + ROPE)
    queries = jnp.concatenate([projected[..., :NOPE], rotate(projected[..., NOPE:], cosine_table[:, None, :], sine_table[:, None, :])], axis=-1).astype(jnp.bfloat16)
    keys_values = jnp.dot(kv_normed, w_kv_up, preferred_element_type=jnp.float32).astype(jnp.bfloat16)
    keys_values = keys_values.reshape(length, HEADS, NOPE + VDIM)
    causal = jnp.arange(length)[:, None] >= jnp.arange(length)[None, :]
    score_scale = (NOPE + ROPE) ** (-0.5)

    def one_head(operands):
        query_head, pair_head = operands
        scores = jnp.dot(query_head[:, :NOPE], pair_head[:, :NOPE].T, preferred_element_type=jnp.float32)
        scores = scores + jnp.dot(query_head[:, NOPE:], key_rope.T, preferred_element_type=jnp.float32)
        scores = jnp.where(causal, scores * score_scale, -jnp.inf)
        weights = jax.nn.softmax(scores, axis=-1).astype(jnp.bfloat16)
        return jnp.dot(weights, pair_head[:, NOPE:], preferred_element_type=jnp.float32).astype(jnp.bfloat16)
    attended = lax.map(one_head, (jnp.transpose(queries, (1, 0, 2)), jnp.transpose(keys_values, (1, 0, 2))))
    return jnp.transpose(attended, (1, 0, 2)).reshape(length, HEADS * VDIM)
```

```python
import functools

import jax
import jax.numpy as jnp
import numpy as np
from jax import lax
from jax.experimental import pallas as pl
from jax.experimental.pallas import tpu as pltpu
from jax.sharding import PartitionSpec as P

ROPE = 64
NOPE = 128
VDIM = 128
Q_LAT = 1536
KV_LAT = 512
SEQ = 1024
GROUP = 16
ROWS = SEQ // GROUP
HEADS = 4
KV_WIDE = KV_LAT + 2 * ROPE
EPSILON = 1e-06
SCORE_SCALE = (NOPE + ROPE) ** (-0.5) * float(np.log2(np.e))
MESH = pl.DeviceIdType.MESH
KV, Q = 0, 1


def angle_table():
    frequency = 10000.0 ** (-np.arange(ROPE // 2) * (2.0 / ROPE))
    angles = np.arange(SEQ)[:, None] * frequency[None, :]
    cosine, sine = np.cos(angles), np.sin(angles)
    table = np.concatenate([cosine, cosine, sine, sine], axis=1) * SCORE_SCALE
    table = table.reshape(4, 2, 2 * ROWS, 2 * ROPE).transpose(1, 0, 2, 3)
    return table.reshape(2, SEQ // 2, 2 * ROPE).astype(np.float32)


def column_map():
    matrix = np.zeros((2 * (NOPE + ROPE), 512), np.float32)
    half = ROPE // 2
    for head in range(2):
        source, target = head * (NOPE + ROPE), head * 256
        for i in range(NOPE + ROPE):
            matrix[source + i, target + i] = 1.0
        for i in range(half):
            matrix[source + NOPE + half + i, target + NOPE + ROPE + i] = -1.0
            matrix[source + NOPE + i, target + NOPE + ROPE + half + i] = 1.0
    return matrix.astype(jnp.bfloat16)


def receive_slots():
    slots = {}
    for kind in (KV, Q):
        for dx in range(4):
            for dh in range(2):
                for dc in range(2):
                    if (dx, dh, dc) == (0, 0, 0):
                        continue
                    subs = (0, 1) if (dx == 2 and dc == 0) else (None,)
                    for sub in subs:
                        slots[(kind, dx, dh, dc, sub)] = len(slots)
    return slots


SLOTS = receive_slots()


def body(
    q_in, kv_in, q_gain, kv_gain, wq_in, wkv_in, table_in, map_in, out,
    q_raw, kv_raw, wq_raw, wq, wkv, table, cmap, q_all, kv_all, keys, values, outs,
    load_sem, send_sem, recv_sem, out_send, out_recv,
):
    me = lax.axis_index("tensor")
    x, h, c = lax.div(me, 4), lax.rem(lax.div(me, 2), 2), lax.rem(me, 2)

    def place(dx, dh, dc):
        x_ = lax.rem(x + dx, 4)
        h_ = h if dh == 0 else 1 - h
        c_ = c if dc == 0 else 1 - c
        return x_, h_, c_

    def index(dx, dh, dc):
        x_, h_, c_ = place(dx, dh, dc)
        return x_ * 4 + h_ * 2 + c_

    def halved(dx, dh, dc):
        x_, h_, c_ = place(dx, dh, dc)
        return h_ * 8 + x_ * 2 + c_

    def block(kind, rel, sub=None):
        first = (index(*rel) if kind == KV else halved(*rel)) * ROWS
        count = ROWS
        if sub is not None:
            first, count = first + sub * (ROWS // 2), ROWS // 2
        ref = kv_all if kind == KV else q_all
        return ref.at[pl.ds(pl.multiple_of(first, 32), count)]

    sent = []

    def send(kind, rel, to, sub=None):
        there = ((rel[0] - to[0]) % 4, rel[1] ^ to[1], rel[2] ^ to[2])
        ref = block(kind, rel, sub)
        copy = pltpu.make_async_remote_copy(
            src_ref=ref, dst_ref=ref, send_sem=send_sem.at[len(sent)],
            recv_sem=recv_sem.at[SLOTS[(kind, *there, sub)]],
            device_id={"tensor": index(*to)}, device_id_type=MESH,
        )
        copy.start()
        sent.append(copy)

    def arrive(kind, rel, sub=None):
        ref = block(kind, rel, sub)
        pltpu.make_async_remote_copy(
            src_ref=ref, dst_ref=ref, send_sem=send_sem.at[0],
            recv_sem=recv_sem.at[SLOTS[(kind, *rel, sub)]],
            device_id={"tensor": index(0, 0, 1)}, device_id_type=MESH,
        ).wait_recv()

    XP, XM, YP, SIB = (1, 0, 0), (3, 0, 0), (0, 1, 0), (0, 0, 1)

    loads = [
        pltpu.make_async_copy(source, target, load_sem.at[i])
        for i, (source, target) in enumerate(
            [(kv_in, kv_raw), (q_in, q_raw), (table_in, table), (wq_in, wq_raw), (map_in, cmap), (wkv_in, wkv)]
        )
    ]
    for load in loads:
        load.start()

    barrier = pltpu.get_barrier_semaphore()
    for peer in range(1, GROUP):
        pl.semaphore_signal(
            barrier, inc=1,
            device_id={"tensor": index(peer // 4, (peer // 2) % 2, peer % 2)}, device_id_type=MESH,
        )

    loads[0].wait()
    loads[2].wait()
    own_kv = block(KV, (0, 0, 0))
    latent = kv_raw[:, :KV_LAT].astype(jnp.float32)
    mean_square = jnp.mean(latent * latent, axis=-1, keepdims=True)
    own_kv[:, :KV_LAT] = (latent * lax.rsqrt(mean_square + EPSILON) * kv_gain[...]).astype(jnp.bfloat16)
    rotary = kv_raw[:, KV_LAT:].astype(jnp.float32)
    swapped = jnp.concatenate([-rotary[:, ROPE // 2 :], rotary[:, : ROPE // 2]], axis=1)
    own_rows = pl.ds(pl.multiple_of((x * 2 + c) * ROWS, ROWS), ROWS)
    angles = table[h, own_rows, :]
    rotated = (rotary * angles[:, :ROPE] + swapped * angles[:, ROPE:]) * (1.0 / SCORE_SCALE)
    rotated = jnp.concatenate([rotated, rotated], axis=1)
    own_kv[:, KV_LAT:] = rotated.astype(jnp.bfloat16)
    loads[1].wait()
    latent = q_raw[...].astype(jnp.float32)
    mean_square = jnp.mean(latent * latent, axis=-1, keepdims=True)
    own_q = block(Q, (0, 0, 0))
    own_q[...] = (latent * lax.rsqrt(mean_square + EPSILON) * q_gain[...]).astype(jnp.bfloat16)

    pl.semaphore_wait(barrier, GROUP - 1)
    for kind in (KV, Q):
        for to in (YP, XP, XM, SIB):
            send(kind, (0, 0, 0), to)

    for head in range(HEADS):
        values[head, :, VDIM:] = jnp.ones((SEQ, 256 - VDIM), jnp.bfloat16)
    loads[3].wait()
    loads[4].wait()
    loads[5].wait()

    def spread(step, _):
        rows = pl.ds(pl.multiple_of(step * 256, 256), 256)
        for pair in range(2):
            wq[rows, pair * 512 : pair * 512 + 512] = jnp.dot(
                wq_raw[rows, pair * 384 : pair * 384 + 384], cmap[...], preferred_element_type=jnp.float32
            ).astype(jnp.bfloat16)
        return 0

    lax.fori_loop(0, Q_LAT // 256, spread, 0)

    def relay_near(kind, dh):
        arrive(kind, (1, dh, 0))
        send(kind, (1, dh, 0), XM, 0)
        send(kind, (1, dh, 0), SIB)
        arrive(kind, (3, dh, 0))
        send(kind, (3, dh, 0), XP, 1)
        send(kind, (3, dh, 0), SIB)

    def relay_far(kind, dh):
        arrive(kind, (2, dh, 0), 0)
        arrive(kind, (2, dh, 0), 1)
        send(kind, (2, dh, 0), SIB)

    def relay_other(kind):
        arrive(kind, YP)
        for to in (XP, XM, SIB):
            send(kind, YP, to)

    relay_near(KV, 0)
    relay_other(KV)
    relay_far(KV, 0)
    relay_near(KV, 1)
    relay_near(Q, 0)
    relay_far(KV, 1)
    for dh in range(2):
        for dx in range(4):
            arrive(KV, (dx, dh, 1))

    def expand(step, _):
        rows = pl.ds(pl.multiple_of(step * 256, 256), 256)
        for head in range(HEADS):
            pair = jnp.dot(
                kv_all[rows, :KV_LAT], wkv[:, head * 256 : head * 256 + 256], preferred_element_type=jnp.float32
            ).astype(jnp.bfloat16)
            keys[head, rows, :NOPE] = pair[:, :NOPE]
            values[head, rows, :VDIM] = pair[:, NOPE:]
            keys[head, rows, NOPE:] = kv_all[rows, KV_LAT:]
        return 0

    lax.fori_loop(0, SEQ // 256, expand, 0)
    relay_far(Q, 0)
    relay_other(Q)
    relay_near(Q, 1)
    relay_far(Q, 1)

    def attend(dh):
        h_ = h if dh == 0 else 1 - h
        row = lax.broadcasted_iota(jnp.int32, (128, 256), 0)
        column = lax.broadcasted_iota(jnp.int32, (128, 256), 1)
        seen = column <= row + h_ * 128

        def one_head(head, _):
            weights = wq[:, pl.ds(pl.multiple_of(head * 256, 256), 256)]
            latents = q_all[pl.ds(pl.multiple_of(h_ * 512, 512), 512), :]
            projected = jnp.dot(latents, weights, preferred_element_type=jnp.float32)
            queries = jnp.concatenate(
                [projected[:, :NOPE] * SCORE_SCALE, projected[:, NOPE:] * table[h_]], axis=1
            ).astype(jnp.bfloat16)
            columns = pl.ds(pl.multiple_of(head * VDIM, VDIM), VDIM)
            for part in range(4):
                last = 256 * (part + 1)
                scores = lax.dot_general(
                    queries[part * 128 : part * 128 + 128], keys[head, :last, :],
                    (((1,), (1,)), ((), ())), preferred_element_type=jnp.float32,
                )
                edge = jnp.where(seen, scores[:, last - 256 :], -jnp.inf)
                scores = edge if part == 0 else jnp.concatenate([scores[:, : last - 256], edge], axis=1)
                highest = jnp.max(scores, axis=1, keepdims=True)
                terms = jnp.exp2(scores - highest).astype(jnp.bfloat16)
                mixed = jnp.dot(terms, values[head, :last, :], preferred_element_type=jnp.float32)
                mixed = mixed[:, :VDIM] / mixed[:, VDIM:]
                rows = pl.ds(pl.multiple_of(h_ * 512 + part * 128, 128), 128)
                outs[rows, columns] = mixed.astype(jnp.bfloat16)
            for dx in range(4):
                for dc in range(2):
                    if (dx, dh, dc) == (0, 0, 0):
                        continue
                    rows = pl.ds(pl.multiple_of(halved(dx, dh, dc) * ROWS, ROWS), ROWS)
                    pltpu.make_async_remote_copy(
                        src_ref=outs.at[rows, columns],
                        dst_ref=out.at[:, pl.ds(pl.multiple_of(me * HEADS * VDIM + head * VDIM, VDIM), VDIM)],
                        send_sem=out_send, recv_sem=out_recv,
                        device_id={"tensor": index(dx, dh, dc)}, device_id_type=MESH,
                    ).start()
            return 0

        lax.fori_loop(0, HEADS, one_head, 0)

    for dx in range(4):
        arrive(Q, (dx, 1, 1))
    attend(1)
    for dx in range(4):
        arrive(Q, (dx, 0, 1))
    attend(0)

    own = pltpu.make_async_copy(
        outs.at[pl.ds(pl.multiple_of(halved(0, 0, 0) * ROWS, ROWS), ROWS)],
        out.at[:, pl.ds(pl.multiple_of(me * HEADS * VDIM, HEADS * VDIM), HEADS * VDIM)],
        load_sem.at[0],
    )
    own.start()
    for copy in sent:
        copy.wait_send()
    own.wait()
    others = (GROUP - 1) * ROWS
    pltpu.make_async_copy(outs.at[pl.ds(0, others)], outs.at[pl.ds(0, others)], out_send).wait()
    width = (GROUP - 1) * HEADS * VDIM
    pltpu.make_async_copy(out.at[:, pl.ds(0, width)], out.at[:, pl.ds(0, width)], out_recv).wait()


def shards(q_latent, kv_latent, q_gain, kv_gain, w_q_up, w_kv_up):
    hbm = pl.BlockSpec(memory_space=pl.ANY)
    vmem = pl.BlockSpec(memory_space=pltpu.VMEM)
    bf16, f32 = jnp.bfloat16, jnp.float32
    return pl.pallas_call(
        body,
        name="latent_attention",
        out_shape=jax.ShapeDtypeStruct((ROWS, GROUP * HEADS * VDIM), bf16),
        in_specs=[hbm, hbm, vmem, vmem, hbm, hbm, hbm, hbm],
        out_specs=hbm,
        scratch_shapes=[
            pltpu.VMEM((ROWS, Q_LAT), bf16),
            pltpu.VMEM((ROWS, KV_LAT + ROPE), bf16),
            pltpu.VMEM((Q_LAT, HEADS * (NOPE + ROPE)), bf16),
            pltpu.VMEM((Q_LAT, HEADS * 256), bf16),
            pltpu.VMEM((KV_LAT, HEADS * 256), bf16),
            pltpu.VMEM((2, SEQ // 2, 2 * ROPE), f32),
            pltpu.VMEM((2 * (NOPE + ROPE), 512), bf16),
            pltpu.VMEM((SEQ, Q_LAT), bf16),
            pltpu.VMEM((SEQ, KV_WIDE), bf16),
            pltpu.VMEM((HEADS, SEQ, 256), bf16),
            pltpu.VMEM((HEADS, SEQ, 256), bf16),
            pltpu.VMEM((SEQ, HEADS * VDIM), bf16),
            pltpu.SemaphoreType.DMA((6,)),
            pltpu.SemaphoreType.DMA((40,)),
            pltpu.SemaphoreType.DMA((len(SLOTS),)),
            pltpu.SemaphoreType.DMA,
            pltpu.SemaphoreType.DMA,
        ],
        compiler_params=pltpu.CompilerParams(
            collective_id=0, has_side_effects=True, vmem_limit_bytes=48 * 2**20
        ),
    )(
        q_latent, kv_latent, q_gain.reshape(1, Q_LAT), kv_gain.reshape(1, KV_LAT), w_q_up, w_kv_up,
        jnp.asarray(angle_table()), jnp.asarray(column_map()),
    )


def solution(mesh):
    return jax.shard_map(
        shards,
        mesh=mesh,
        in_specs=(
            P(("dp", "tensor"), None),
            P(("dp", "tensor"), None),
            P(),
            P(),
            P(None, "tensor"),
            P(None, "tensor"),
        ),
        out_specs=P(("dp", "tensor"), None),
        check_vma=False,
    )
```
